512 devices in a mesh: occ: 32 (over z_lo, x, core), vir: 16 (over y, z_hi).
Axes of the slice: x: 4, y: 4, z: 16 (z_hi: 4, z_lo: 4; z = z_hi * 4 + z_lo), core: 2. Of those that a mesh axis runs over, the one named last changes fastest.
Arguments:
- amplitudes: float32 [4864, 2560], P('occ', 'vir'), may hold values from -6 to 6
- integrals: float32 [2560, 16384], P('occ', 'vir'), may hold values from -0.125 to 0.125
- pair_list: int32 [4864, 2], P('occ'), may hold values from 0 to 99, as said below
- partner: int32 [2560], replicated, may hold values from 0 to 2559, as said below
Outputs:
- ladder: float32 [4864, 16384], P('occ', 'vir')
The draws below stay inside these ranges and needn't reach their ends.
Inputs may be any that keep to these rules, and one draw needn't show every extreme that they name: `pair_list`: the rows are distinct pairs with i <= j, a subset of all pairs of 100 occupied orbitals; some rows have i == j. partner[partner[k]] == k and partner[k] != k for every slot k.
All inputs are finite; a program needn't handle non-finite values.
Results may differ from the reference program's by a relative error of at most 0.00007.
Values sent between devices are 32-bit elements; how exact they have to be, the bound alone decides.
No kernel may reach another device: no remote copies, remote signals or barrier semaphores. Data moves between devices by JAX's collectives and lax.ppermute only.
A program may use at most 64 MiB of HBM per device.

```python
import jax
import jax.numpy as jnp
import numpy as np
from jax import lax

CD = 2560
NO = 100
NA = 128
IJ = 4864
AB = 16384


def draw_pair_list(key, part):
    key = jax.random.fold_in(key, 11)
    first_rows, second_rows = np.triu_indices(NO)
    total_pairs = first_rows.shape[0]
    shuffled = jax.random.permutation(key, total_pairs - 2) + 1
    chosen = jnp.concatenate([jnp.array([0, total_pairs - 1], jnp.int32), shuffled.astype(jnp.int32)])[:IJ]
    smaller = jnp.take(jnp.asarray(first_rows, jnp.int32), chosen)
    larger = jnp.take(jnp.asarray(second_rows, jnp.int32), chosen)
    return jnp.stack([smaller, larger], axis=1).astype(jnp.int32)


def draw_partner(key, part):
    key = jax.random.fold_in(key, 23)
    shuffled = jax.random.permutation(key, CD)
    flipped = shuffled.reshape(CD // 2, 2)[:, ::-1].reshape(CD)
    inverse = jnp.argsort(shuffled)
    return flipped[inverse].astype(jnp.int32)


def block_scale(own_key, extent, shards, low, top_value):
    def one(position, shards_of):
        draws = jax.random.uniform(jax.random.fold_in(jax.random.fold_in(own_key, 6), position), (shards_of,), jnp.float32, low / len(shards), top_value / len(shards))
        return jnp.repeat(jnp.exp(draws), extent[position] // shards_of).reshape((-1,) + (1,) * (len(extent) - position - 1))

    loudness = one(*shards[0])
    for cut in shards[1:]:
        loudness = loudness * one(*cut)
    return loudness


def normal_values(stream_key, dims, spread, limit, split=(), held_as=jnp.bfloat16):
    factor_of = block_scale(stream_key, dims, split, -0.22, 0.18) if split else 1.0
    result = jax.random.normal(stream_key, dims, jnp.float32) * spread * factor_of
    return jnp.minimum(jnp.maximum(result, -limit), limit).astype(held_as)


def setup_inputs(seed: int = 0) -> dict:
    seeds = jax.random.split(jax.random.key(seed), 5)
    amplitudes = normal_values(seeds[0], (IJ, CD), 1.0, 6.0, ((0, 32), (1, 16)), jnp.float32)
    integrals = normal_values(seeds[1], (CD, AB), CD ** -0.5, 0.125, ((0, 32), (1, 16)), jnp.float32)
    pair_list = draw_pair_list(jax.random.fold_in(seeds[4], 71), 0)
    partner = draw_partner(jax.random.fold_in(seeds[4], 71), 0)
    return dict(amplitudes=amplitudes, integrals=integrals, pair_list=pair_list, partner=partner)


def reference(amplitudes, integrals, pair_list, partner):
    antisym = amplitudes - jnp.take(amplitudes, partner, axis=1)
    direct = jnp.dot(antisym, integrals, precision=lax.Precision.HIGHEST, preferred_element_type=jnp.float32)
    weight = jnp.where(pair_list[:, 0] == pair_list[:, 1], 0.5, 1.0).astype(jnp.float32)
    square = direct.reshape(direct.shape[0], NA, NA)
    ladder = weight[:, None, None] * (square + jnp.swapaxes(square, 1, 2))
    return ladder.reshape(direct.shape[0], NA * NA)
```

```python
import jax
import jax.numpy as jnp
from jax import lax
from jax.sharding import Mesh, PartitionSpec as P

NA = 128
VIR = ("y", "zh")
OCC = ("zl", "x", "c")
RING = (0, 1, 3, 2)
SLOT = (0, 2, 3, 1)


def shift(n, by):
    return [(i, (i + by) % n) for i in range(n)]


def both_ways(block, axis):
    half = block.shape[0] // 2
    left = lax.ppermute(block, axis, shift(4, 1))
    right = lax.ppermute(block, axis, shift(4, -1))
    far_top = lax.ppermute(left[:half], axis, shift(4, 1))
    far_low = lax.ppermute(right[half:], axis, shift(4, -1))
    return [block, left, right, far_top, far_low]


def symmetrized(integrals):
    rows = integrals.shape[0]
    here = integrals.shape[1] // NA
    ranks = NA // here
    sent = integrals.reshape(rows, here, ranks, here).transpose(2, 1, 3, 0).reshape(ranks, here, here * rows)
    got = lax.all_to_all(sent, VIR, split_axis=0, concat_axis=0, tiled=True)
    swapped = got.reshape(NA, here * rows).T.reshape(here, rows, NA)
    return integrals + swapped.transpose(1, 0, 2).reshape(integrals.shape)


def body(amplitudes, integrals, pair_list, partner):
    rows_k = integrals.shape[0]
    x, core = lax.axis_index("x"), lax.axis_index("c")
    y, zh = lax.axis_index("y"), lax.axis_index("zh")
    ring_place = jnp.array([0, 1, 3, 2], jnp.int32)[lax.axis_index("zl")]

    blocks = [symmetrized(integrals)]
    for _ in range(3):
        blocks.append(lax.ppermute(blocks[-1], "zl", [(RING[i], RING[(i + 1) % 4]) for i in range(4)]))
    slabs = [jnp.concatenate(both_ways(b, "x"), axis=0) for b in blocks]

    columns_k = amplitudes.shape[1]
    by_zh = jnp.concatenate(both_ways(amplitudes.T, "zh"), axis=0)
    tau = jnp.concatenate(both_ways(by_zh, "y"), axis=0)

    ring = jnp.array(RING, jnp.int32)
    zs = ring[(ring_place - jnp.arange(4)) % 4]
    xs = (x + jnp.array([0, -1, 1, 2])) % 4
    chunk = (zs[:, None] * 4 + xs[None, :]).reshape(16) * 2
    chunk = jnp.concatenate([chunk + core, chunk + 1 - core])
    slot = jnp.array(SLOT, jnp.int32)

    def place(k):
        rank = k // columns_k
        return (slot[(rank // 4 - y) % 4] * 4 + slot[(rank % 4 - zh) % 4]) * columns_k + k % columns_k

    own = (chunk[:, None] * rows_k + jnp.arange(rows_k)[None, :]).reshape(-1)
    other = partner.reshape(-1, rows_k).at[chunk].get(mode="promise_in_bounds").reshape(-1)
    antisym = tau.at[place(own)].get(mode="promise_in_bounds") - tau.at[place(other)].get(mode="promise_in_bounds")
    half = antisym.shape[0] // 2
    mine = antisym[:half]
    theirs = lax.ppermute(antisym[half:], "c", shift(2, 1))

    def product(lhs):
        return lax.dot_general(
            lhs, jnp.concatenate(slabs, axis=0), (((0,), (0,)), ((), ())),
            precision=lax.Precision.HIGH, preferred_element_type=jnp.float32,
        )

    back = lax.ppermute(product(theirs), "c", shift(2, 1))
    weight = jnp.where(pair_list[:, 0] == pair_list[:, 1], 0.5, 1.0).astype(jnp.float32)
    return weight[:, None] * (product(mine) + back)


def solution(mesh):
    fine = Mesh(mesh.devices.reshape(4, 4, 2, 4, 4), OCC + VIR)
    placed = (P(OCC, VIR), P(OCC, VIR), P(OCC, None), P())
    return jax.shard_map(
        body, mesh=fine, in_specs=placed, out_specs=P(OCC, VIR), check_vma=False
    )
```

```python
import functools

import jax
import jax.numpy as jnp
from jax import lax
from jax.experimental import pallas as pl
from jax.experimental.pallas import tpu as pltpu
from jax.sharding import Mesh, PartitionSpec as P

NA = 128
VIR = ("y", "zh")
OCC = ("zl", "x", "c")
RING = (0, 1, 3, 2)
SLOT = (0, 2, 3, 1)
VMEM = pl.BlockSpec(memory_space=pltpu.VMEM)
SMEM = pl.BlockSpec(memory_space=pltpu.SMEM)


def shift(n, by):
    return [(i, (i + by) % n) for i in range(n)]


def around(up, down, axis):
    return lax.ppermute(up, axis, shift(4, 1)), lax.ppermute(down, axis, shift(4, -1))


def symmetrized(integrals):
    rows = integrals.shape[0]
    here = integrals.shape[1] // NA
    ranks = NA // here
    sent = integrals.reshape(rows, here, ranks, here).transpose(2, 1, 3, 0).reshape(ranks, here, here * rows)
    got = lax.all_to_all(sent, VIR, split_axis=0, concat_axis=0, tiled=True)
    swapped = got.reshape(NA, here * rows).T.reshape(here, rows, NA)
    return integrals + swapped.transpose(1, 0, 2).reshape(integrals.shape)


def antisym_kernel(block, base_ref, other_ref, tau_ref, mine_ref, theirs_ref, rows_ref):
    total = rows_ref.shape[0]

    def one(b, _):
        at = pl.multiple_of(b * block, 8)
        for r in range(block):
            rows_ref[pl.ds(at + r, 1), :] = tau_ref[pl.ds(other_ref[at + r], 1), :]
        here = tau_ref[pl.ds(pl.multiple_of(base_ref[b], 8), block), :]
        rows_ref[pl.ds(at, block), :] = here - rows_ref[pl.ds(at, block), :]
        return 0

    lax.fori_loop(0, total // block, one, 0)
    half = total // 2
    for j in range(0, half, 128):
        mine_ref[:, j : j + 128] = rows_ref[j : j + 128, :].T
        theirs_ref[:, j : j + 128] = rows_ref[half + j : half + j + 128, :].T


def product_kernel(counts, mine_ref, theirs_ref, *refs):
    pieces = refs[: len(counts)]
    own_ref, other_ref, high_ref, low_ref = refs[len(counts) :]
    at = 0
    for piece, count in zip(pieces, counts):
        for r in range(0, count, 80):
            value = piece[r : r + 80, :]
            high = value.astype(jnp.bfloat16)
            high_ref[at : at + 80, :] = high
            low_ref[at : at + 80, :] = (value - high.astype(jnp.float32)).astype(jnp.bfloat16)
            at += 80
    lhs = jnp.concatenate([mine_ref[...], theirs_ref[...]], axis=0)
    lhs_high = lhs.astype(jnp.bfloat16)
    lhs_low = (lhs - lhs_high.astype(jnp.float32)).astype(jnp.bfloat16)
    dot = functools.partial(jnp.dot, preferred_element_type=jnp.float32)
    pairs = own_ref.shape[0]
    for n in range(0, own_ref.shape[1], 256):
        high, low = high_ref[:, n : n + 256], low_ref[:, n : n + 256]
        total = dot(lhs_high, high) + (dot(lhs_high, low) + dot(lhs_low, high))
        own_ref[:, n : n + 256] = total[:pairs]
        other_ref[:, n : n + 256] = total[pairs:]


def body(amplitudes, integrals, pair_list, partner):
    rows_k, columns = integrals.shape
    pairs, columns_k = amplitudes.shape
    slab = partner.shape[0]
    x, core = lax.axis_index("x"), lax.axis_index("c")
    zh = lax.axis_index("zh")
    ring_place = jnp.array([0, 1, 3, 2], jnp.int32)[lax.axis_index("zl")]

    s = [symmetrized(integrals)]
    for _ in range(3):
        s.append(lax.ppermute(s[-1], "zl", [(RING[i], RING[(i + 1) % 4]) for i in range(4)]))
    first = jnp.concatenate(s[:2], axis=0)
    la, ra = around(first, first, "x")
    lb, rb = around(
        jnp.concatenate([s[2], s[3], la[:rows_k]], axis=0), jnp.concatenate([s[2], s[3], ra[rows_k:]], axis=0), "x"
    )
    lc, rc = around(lb[:rows_k], rb[rows_k : 2 * rows_k], "x")
    pieces = s + [la, ra, lb, rb, lc, rc]
    order = [(0, 0), (1, 0), (2, 0), (3, 0), (0, -1), (1, -1), (0, 1), (1, 1)]
    order += [(2, -1), (3, -1), (0, 2), (2, 1), (3, 1), (1, 2), (2, 2), (3, 2)]

    turned = amplitudes.T
    half = columns_k // 2
    left, right = around(turned, turned, "zh")
    far_top, far_low = around(left[:half], right[half:], "zh")
    by_zh = jnp.concatenate([turned, left, right, far_top, far_low], axis=0)
    tau = lax.all_gather(by_zh, "y", axis=0, tiled=True)

    slot = jnp.array(SLOT, jnp.int32)

    def place(k):
        rank = k // columns_k
        return ((rank // 4) * 4 + slot[(rank % 4 - zh) % 4]) * columns_k + k % columns_k

    steps = jnp.array(order, jnp.int32)
    zs = jnp.array(RING, jnp.int32)[(ring_place - steps[:, 0]) % 4]
    chunk = (zs * 4 + (x + steps[:, 1]) % 4) * 2
    chunk = jnp.concatenate([chunk + core, chunk + 1 - core])
    base = place(chunk * rows_k)
    other = place(partner).reshape(-1, rows_k).at[chunk].get(mode="promise_in_bounds").reshape(-1)
    mine, theirs = pl.pallas_call(
        functools.partial(antisym_kernel, rows_k),
        out_shape=[jax.ShapeDtypeStruct((pairs, slab // 2), jnp.float32)] * 2,
        in_specs=[SMEM, SMEM, VMEM],
        out_specs=[VMEM] * 2,
        scratch_shapes=[pltpu.VMEM((slab, pairs), jnp.float32)],
        compiler_params=pltpu.CompilerParams(vmem_limit_bytes=16 * 2**20),
        cost_estimate=pl.CostEstimate(flops=slab * pairs, bytes_accessed=3 * slab * pairs * 4, transcendentals=0),
        name="antisym",
    )(base, other, tau)
    theirs = lax.ppermute(theirs, "c", shift(2, 1))

    own, back = pl.pallas_call(
        functools.partial(product_kernel, [p.shape[0] for p in pieces]),
        out_shape=[jax.ShapeDtypeStruct((pairs, columns), jnp.float32)] * 2,
        in_specs=[VMEM] * (2 + len(pieces)),
        out_specs=[VMEM] * 2,
        scratch_shapes=[pltpu.VMEM((slab // 2, columns), jnp.bfloat16)] * 2,
        compiler_params=pltpu.CompilerParams(vmem_limit_bytes=32 * 2**20),
        cost_estimate=pl.CostEstimate(flops=6 * pairs * slab * columns, bytes_accessed=8 * 2**20, transcendentals=0),
        name="product",
    )(mine, theirs, *pieces)
    back = lax.ppermute(back, "c", shift(2, 1))
    weight = jnp.where(pair_list[:, 0] == pair_list[:, 1], 0.5, 1.0).astype(jnp.float32)
    return weight[:, None] * (own + back)


def solution(mesh):
    fine = Mesh(mesh.devices.reshape(4, 4, 2, 4, 4), OCC + VIR)
    placed = (P(OCC, VIR), P(OCC, VIR), P(OCC, None), P())
    return jax.shard_map(
        body, mesh=fine, in_specs=placed, out_specs=P(OCC, VIR), check_vma=False
    )
```

```python
import functools

import jax
import jax.numpy as jnp
from jax import lax
from jax.experimental import pallas as pl
from jax.experimental.pallas import tpu as pltpu
from jax.sharding import Mesh, PartitionSpec as P

NA = 128
VIR = ("y", "zh")
OCC = ("zl", "x", "c")
RING = (0, 1, 3, 2)
SLOT = (0, 2, 3, 1)
VMEM = pl.BlockSpec(memory_space=pltpu.VMEM)
SMEM = pl.BlockSpec(memory_space=pltpu.SMEM)


def shift(n, by):
    return [(i, (i + by) % n) for i in range(n)]


def pack_kernel(turned_ref, packed_ref):
    rows, pairs = turned_ref.shape
    tail = pairs - 128
    step = packed_ref.shape[0] - rows
    packed_ref[:rows, :] = turned_ref[:, :128]
    parts = [turned_ref[j : j + step, 128:] for j in range(0, rows, step)]
    parts.append(jnp.zeros((step, 128 - tail * len(parts)), jnp.float32))
    packed_ref[rows:, :] = jnp.concatenate(parts, axis=1)


def symmetrize_kernel(integrals_ref, got_ref, out_ref, turned_ref):
    ranks, here = got_ref.shape[0], integrals_ref.shape[1] // NA
    rows = integrals_ref.shape[0]
    for t in range(here * rows // 128):
        block = got_ref[:, t * here : (t + 1) * here, :].reshape(ranks * here, 128)
        turned_ref[t * 128 : (t + 1) * 128, :] = block.T
    for a in range(here):
        columns = slice(a * NA, (a + 1) * NA)
        out_ref[:, columns] = integrals_ref[:, columns] + turned_ref[a * rows : (a + 1) * rows, :]


def copies_kernel(*refs):
    copies_ref = refs[-1]
    at = 0
    for piece in refs[:-1]:
        for i in range(copies_ref.shape[0]):
            copies_ref[i, at : at + piece.shape[0], :] = piece[...]
        at += piece.shape[0]


def antisym_kernel(block, columns_k, base_ref, other_ref, tau_ref, mine_ref, theirs_ref, head_ref, tail_ref, rows_ref, ends_ref):
    total = rows_ref.shape[0]
    pairs = mine_ref.shape[0]
    ranks = total // columns_k
    per = tau_ref.shape[0] // ranks
    step = per - columns_k
    for r in range(ranks):
        head_ref[r * columns_k : (r + 1) * columns_k, :] = tau_ref[r * per : r * per + columns_k, :]
        packed = tau_ref[r * per + columns_k : (r + 1) * per, :]
        for j in range(columns_k // step):
            turned = packed if j == 0 else pltpu.roll(packed, 128 - j * (pairs - 128), 1)
            tail_ref[r * columns_k + j * step : r * columns_k + (j + 1) * step, :] = turned

    def one(b, _):
        at = pl.multiple_of(b * block, 8)
        for r in range(block):
            k = other_ref[at + r]
            rows_ref[pl.ds(at + r, 1), :] = head_ref[pl.ds(k, 1), :]
            ends_ref[pl.ds(at + r, 1), :] = tail_ref[pl.ds(k, 1), :]
        here = pl.ds(pl.multiple_of(base_ref[b], 8), block)
        rows_ref[pl.ds(at, block), :] = head_ref[here, :] - rows_ref[pl.ds(at, block), :]
        ends_ref[pl.ds(at, block), :] = tail_ref[here, :] - ends_ref[pl.ds(at, block), :]
        return 0

    lax.fori_loop(0, total // block, one, 0)
    half = total // 2
    for j in range(0, half, 128):
        mine_ref[:128, j : j + 128] = rows_ref[j : j + 128, :].T
        mine_ref[128:, j : j + 128] = ends_ref[j : j + 128, :].T[: pairs - 128]
        theirs_ref[:128, j : j + 128] = rows_ref[half + j : half + j + 128, :].T
        theirs_ref[128:, j : j + 128] = ends_ref[half + j : half + j + 128, :].T[: pairs - 128]


def product_kernel(counts, mine_ref, theirs_ref, *refs):
    pieces = refs[: len(counts)]
    own_ref, other_ref, high_ref, low_ref = refs[len(counts) :]
    at = 0
    for piece, count in zip(pieces, counts):
        for r in range(0, count, 80):
            value = piece[r : r + 80, :]
            high = value.astype(jnp.bfloat16)
            high_ref[at : at + 80, :] = high
            low_ref[at : at + 80, :] = (value - high.astype(jnp.float32)).astype(jnp.bfloat16)
            at += 80
    lhs = jnp.concatenate([mine_ref[...], theirs_ref[...]], axis=0)
    lhs_high = lhs.astype(jnp.bfloat16)
    lhs_low = (lhs - lhs_high.astype(jnp.float32)).astype(jnp.bfloat16)
    dot = functools.partial(jnp.dot, preferred_element_type=jnp.float32)
    pairs = own_ref.shape[0]
    for n in range(0, own_ref.shape[1], 256):
        high, low = high_ref[:, n : n + 256], low_ref[:, n : n + 256]
        total = dot(lhs_high, high) + (dot(lhs_high, low) + dot(lhs_low, high))
        own_ref[:, n : n + 256] = total[:pairs]
        other_ref[:, n : n + 256] = total[pairs:]


def around(up, down, axis):
    return lax.ppermute(up, axis, shift(4, 1)), lax.ppermute(down, axis, shift(4, -1))


def body(amplitudes, integrals, pair_list, partner):
    rows_k, columns = integrals.shape
    pairs, columns_k = amplitudes.shape
    slab = partner.shape[0]
    x, core, zh = lax.axis_index("x"), lax.axis_index("c"), lax.axis_index("zh")
    ring_place = jnp.array([0, 1, 3, 2], jnp.int32)[lax.axis_index("zl")]

    lanes = 128 // (pairs - 128)
    packed_rows = columns_k + columns_k // lanes
    packed = pl.pallas_call(
        pack_kernel,
        out_shape=jax.ShapeDtypeStruct((packed_rows, 128), jnp.float32),
        in_specs=[VMEM],
        out_specs=VMEM,
        name="pack",
    )(amplitudes.T)
    left, right = around(packed, packed, "zh")
    half = packed_rows // 2
    far = around(left[:half], right[half:], "zh")
    copies = pl.pallas_call(
        copies_kernel,
        out_shape=jax.ShapeDtypeStruct((4, 4 * packed_rows, 128), jnp.float32),
        in_specs=[VMEM] * 5,
        out_specs=VMEM,
        name="copies",
    )(packed, left, right, *far)
    tau = lax.all_to_all(copies, "y", split_axis=0, concat_axis=0, tiled=True).reshape(-1, 128)

    here = columns // NA
    ranks = NA // here
    tiles = here * rows_k // 128
    blocks = integrals.reshape(rows_k, here, ranks, here).transpose(2, 1, 3, 0).reshape(ranks, here, tiles, 128)
    sent = blocks.transpose(0, 2, 1, 3).reshape(ranks, tiles * here, 128)
    got = lax.all_to_all(sent, VIR, split_axis=0, concat_axis=0, tiled=True)
    start = pl.pallas_call(
        symmetrize_kernel,
        out_shape=jax.ShapeDtypeStruct((rows_k, columns), jnp.float32),
        in_specs=[VMEM] * 2,
        out_specs=VMEM,
        scratch_shapes=[pltpu.VMEM((tiles * 128, 128), jnp.float32)],
        name="symmetrize",
    )(integrals, got)

    s = [start]
    for _ in range(3):
        s.append(lax.ppermute(s[-1], "zl", [(RING[i], RING[(i + 1) % 4]) for i in range(4)]))
    pieces, order = [], []
    for i in (0, 2):
        part = jnp.concatenate(s[i : i + 2], axis=0)
        left, right = around(part, part, "x")
        pieces += [part, left, right, *around(left[:rows_k], right[rows_k:], "x")]
        order += [(i, 0), (i + 1, 0), (i, -1), (i + 1, -1), (i, 1), (i + 1, 1), (i, 2), (i + 1, 2)]

    slot = jnp.array(SLOT, jnp.int32)

    def place(k):
        rank = k // columns_k
        return ((rank // 4) * 4 + slot[(rank % 4 - zh) % 4]) * columns_k + k % columns_k

    steps = jnp.array(order, jnp.int32)
    zs = jnp.array(RING, jnp.int32)[(ring_place - steps[:, 0]) % 4]
    chunk = (zs * 4 + (x + steps[:, 1]) % 4) * 2
    chunk = jnp.concatenate([chunk + core, chunk + 1 - core])
    other = place(partner).reshape(-1, rows_k).at[chunk].get(mode="promise_in_bounds").reshape(-1)
    mine, theirs = pl.pallas_call(
        functools.partial(antisym_kernel, rows_k, columns_k),
        out_shape=[jax.ShapeDtypeStruct((pairs, slab // 2), jnp.float32)] * 2,
        in_specs=[SMEM, SMEM, VMEM],
        out_specs=[VMEM] * 2,
        scratch_shapes=[pltpu.VMEM((slab, 128), jnp.float32)] * 4,
        compiler_params=pltpu.CompilerParams(vmem_limit_bytes=16 * 2**20),
        cost_estimate=pl.CostEstimate(flops=slab * pairs, bytes_accessed=3 * slab * pairs * 4, transcendentals=0),
        name="antisym",
    )(place(chunk * rows_k), other, tau)
    theirs = lax.ppermute(theirs, "c", shift(2, 1))

    own, back = pl.pallas_call(
        functools.partial(product_kernel, [p.shape[0] for p in pieces]),
        out_shape=[jax.ShapeDtypeStruct((pairs, columns), jnp.float32)] * 2,
        in_specs=[VMEM] * (2 + len(pieces)),
        out_specs=[VMEM] * 2,
        scratch_shapes=[pltpu.VMEM((slab // 2, columns), jnp.bfloat16)] * 2,
        compiler_params=pltpu.CompilerParams(vmem_limit_bytes=32 * 2**20),
        cost_estimate=pl.CostEstimate(flops=6 * pairs * slab * columns, bytes_accessed=8 * 2**20, transcendentals=0),
        name="product",
    )(mine, theirs, *pieces)
    back = lax.ppermute(back, "c", shift(2, 1))
    weight = jnp.where(pair_list[:, 0] == pair_list[:, 1], 0.5, 1.0).astype(jnp.float32)
    return weight[:, None] * (own + back)


def solution(mesh):
    fine = Mesh(mesh.devices.reshape(4, 4, 2, 4, 4), OCC + VIR)
    placed = (P(OCC, VIR), P(OCC, VIR), P(OCC, None), P())
    return jax.shard_map(
        body, mesh=fine, in_specs=placed, out_specs=P(OCC, VIR), check_vma=False
    )
```

```python
import functools

import jax
import jax.numpy as jnp
from jax import lax
from jax.experimental import pallas as pl
from jax.experimental.pallas import tpu as pltpu
from jax.sharding import Mesh, PartitionSpec as P

NA = 128
VIR = ("y", "zh")
OCC = ("zl", "x", "c")
RING = (0, 1, 3, 2)
SLOT = (0, 2, 3, 1)
VMEM = pl.BlockSpec(memory_space=pltpu.VMEM)
SMEM = pl.BlockSpec(memory_space=pltpu.SMEM)


def shift(n, by):
    return [(i, (i + by) % n) for i in range(n)]


def pack_kernel(turned_ref, packed_ref):
    rows, pairs = turned_ref.shape
    tail = pairs - 128
    step = packed_ref.shape[0] - rows
    packed_ref[:rows, :] = turned_ref[:, :128]
    parts = [turned_ref[j : j + step, 128:] for j in range(0, rows, step)]
    parts.append(jnp.zeros((step, 128 - tail * len(parts)), jnp.float32))
    packed_ref[rows:, :] = jnp.concatenate(parts, axis=1)


def symmetrize_kernel(integrals_ref, got_ref, out_ref, turned_ref):
    ranks, here = got_ref.shape[0], integrals_ref.shape[1] // NA
    rows = integrals_ref.shape[0]
    for t in range(here * rows // 128):
        block = got_ref[:, t * here : (t + 1) * here, :].reshape(ranks * here, 128)
        turned_ref[t * 128 : (t + 1) * 128, :] = block.T
    for a in range(here):
        columns = slice(a * NA, (a + 1) * NA)
        out_ref[:, columns] = integrals_ref[:, columns] + turned_ref[a * rows : (a + 1) * rows, :]


def copies_kernel(*refs):
    copies_ref = refs[-1]
    at = 0
    for piece in refs[:-1]:
        for i in range(copies_ref.shape[0]):
            copies_ref[i, at : at + piece.shape[0], :] = piece[...]
        at += piece.shape[0]


def antisym_kernel(block, columns_k, chunk_ref, base_ref, other_ref, tau_ref, mine_ref, theirs_ref, head_ref, tail_ref, rows_ref, ends_ref):
    total = rows_ref.shape[0]
    pairs = mine_ref.shape[0]
    ranks = total // columns_k
    per = tau_ref.shape[0] // ranks
    step = per - columns_k
    for r in range(ranks):
        head_ref[r * columns_k : (r + 1) * columns_k, :] = tau_ref[r * per : r * per + columns_k, :]
        packed = tau_ref[r * per + columns_k : (r + 1) * per, :]
        for j in range(columns_k // step):
            turned = packed if j == 0 else pltpu.roll(packed, 128 - j * (pairs - 128), 1)
            tail_ref[r * columns_k + j * step : r * columns_k + (j + 1) * step, :] = turned

    def one(b, _):
        at = pl.multiple_of(b * block, 8)
        first = chunk_ref[b]
        for r in range(block):
            k = other_ref[first + r]
            rows_ref[pl.ds(at + r, 1), :] = head_ref[pl.ds(k, 1), :]
            ends_ref[pl.ds(at + r, 1), :] = tail_ref[pl.ds(k, 1), :]
        here = pl.ds(pl.multiple_of(base_ref[b], 8), block)
        rows_ref[pl.ds(at, block), :] = head_ref[here, :] - rows_ref[pl.ds(at, block), :]
        ends_ref[pl.ds(at, block), :] = tail_ref[here, :] - ends_ref[pl.ds(at, block), :]
        return 0

    lax.fori_loop(0, total // block, one, 0)
    half = total // 2
    for j in range(0, half, 128):
        mine_ref[:128, j : j + 128] = rows_ref[j : j + 128, :].T
        mine_ref[128:, j : j + 128] = ends_ref[j : j + 128, :].T[: pairs - 128]
        theirs_ref[:128, j : j + 128] = rows_ref[half + j : half + j + 128, :].T
        theirs_ref[128:, j : j + 128] = ends_ref[half + j : half + j + 128, :].T[: pairs - 128]


def product_kernel(counts, mine_ref, theirs_ref, *refs):
    pieces = refs[: len(counts)]
    own_ref, other_ref, high_ref, low_ref = refs[len(counts) :]
    at = 0
    for piece, count in zip(pieces, counts):
        for r in range(0, count, 80):
            value = piece[r : r + 80, :]
            high = value.astype(jnp.bfloat16)
            high_ref[at : at + 80, :] = high
            low_ref[at : at + 80, :] = (value - high.astype(jnp.float32)).astype(jnp.bfloat16)
            at += 80
    lhs = jnp.concatenate([mine_ref[...], theirs_ref[...]], axis=0)
    lhs_high = lhs.astype(jnp.bfloat16)
    lhs_low = (lhs - lhs_high.astype(jnp.float32)).astype(jnp.bfloat16)
    dot = functools.partial(jnp.dot, preferred_element_type=jnp.float32)
    pairs = own_ref.shape[0]
    for n in range(0, own_ref.shape[1], 256):
        high, low = high_ref[:, n : n + 256], low_ref[:, n : n + 256]
        total = dot(lhs_high, high) + (dot(lhs_high, low) + dot(lhs_low, high))
        own_ref[:, n : n + 256] = total[:pairs]
        other_ref[:, n : n + 256] = total[pairs:]


def around(up, down, axis):
    return lax.ppermute(up, axis, shift(4, 1)), lax.ppermute(down, axis, shift(4, -1))


def body(amplitudes, integrals, pair_list, partner):
    rows_k, columns = integrals.shape
    pairs, columns_k = amplitudes.shape
    slab = partner.shape[0]
    x, core, zh = lax.axis_index("x"), lax.axis_index("c"), lax.axis_index("zh")
    ring_place = jnp.array([0, 1, 3, 2], jnp.int32)[lax.axis_index("zl")]

    lanes = 128 // (pairs - 128)
    packed_rows = columns_k + columns_k // lanes
    packed = pl.pallas_call(
        pack_kernel,
        out_shape=jax.ShapeDtypeStruct((packed_rows, 128), jnp.float32),
        in_specs=[VMEM],
        out_specs=VMEM,
        compiler_params=pltpu.CompilerParams(vmem_limit_bytes=8 * 2**20),
        name="pack",
    )(amplitudes.T)
    left, right = around(packed, packed, "zh")
    half = packed_rows // 2
    far = around(left[:half], right[half:], "zh")
    copies = pl.pallas_call(
        copies_kernel,
        out_shape=jax.ShapeDtypeStruct((4, 4 * packed_rows, 128), jnp.float32),
        in_specs=[VMEM] * 5,
        out_specs=VMEM,
        compiler_params=pltpu.CompilerParams(vmem_limit_bytes=8 * 2**20),
        name="copies",
    )(packed, left, right, *far)
    tau = lax.all_to_all(copies, "y", split_axis=0, concat_axis=0, tiled=True).reshape(-1, 128)

    here = columns // NA
    ranks = NA // here
    tiles = here * rows_k // 128
    blocks = integrals.reshape(rows_k, here, ranks, here).transpose(2, 1, 3, 0).reshape(ranks, here, tiles, 128)
    sent = blocks.transpose(0, 2, 1, 3).reshape(ranks, tiles * here, 128)
    got = lax.all_to_all(sent, VIR, split_axis=0, concat_axis=0, tiled=True)
    start = pl.pallas_call(
        symmetrize_kernel,
        out_shape=jax.ShapeDtypeStruct((rows_k, columns), jnp.float32),
        in_specs=[VMEM] * 2,
        out_specs=VMEM,
        scratch_shapes=[pltpu.VMEM((tiles * 128, 128), jnp.float32)],
        compiler_params=pltpu.CompilerParams(vmem_limit_bytes=8 * 2**20),
        name="symmetrize",
    )(integrals, got)

    def lower(block):
        return lax.ppermute(block, "zl", [(RING[i], RING[(i + 1) % 4]) for i in range(4)])

    one = lower(start)
    two = lower(one)
    first = jnp.concatenate([start, one], axis=0)
    first = [first, *around(first, first, "x")]
    three = lower(two)
    last = jnp.concatenate([two, three], axis=0)
    last = [last, *around(last, last, "x")]
    pieces, order = [], []
    for i, part in ((0, first), (2, last)):
        pieces += part + list(around(part[1][:rows_k], part[2][rows_k:], "x"))
        order += [(i, 0), (i + 1, 0), (i, -1), (i + 1, -1), (i, 1), (i + 1, 1), (i, 2), (i + 1, 2)]

    slot = jnp.array(SLOT, jnp.int32)

    def place(k):
        rank = k // columns_k
        return k + (slot[(rank % 4 - zh) % 4] - rank % 4) * columns_k

    steps = jnp.array(order, jnp.int32)
    zs = jnp.array(RING, jnp.int32)[(ring_place - steps[:, 0]) % 4]
    chunk = (zs * 4 + (x + steps[:, 1]) % 4) * 2
    chunk = jnp.concatenate([chunk + core, chunk + 1 - core]) * rows_k
    mine, theirs = pl.pallas_call(
        functools.partial(antisym_kernel, rows_k, columns_k),
        out_shape=[jax.ShapeDtypeStruct((pairs, slab // 2), jnp.float32)] * 2,
        in_specs=[SMEM, SMEM, SMEM, VMEM],
        out_specs=[VMEM] * 2,
        scratch_shapes=[pltpu.VMEM((slab, 128), jnp.float32)] * 4,
        compiler_params=pltpu.CompilerParams(vmem_limit_bytes=10 * 2**20),
        cost_estimate=pl.CostEstimate(flops=slab * pairs, bytes_accessed=3 * slab * pairs * 4, transcendentals=0),
        name="antisym",
    )(chunk, place(chunk), place(partner), tau)
    theirs = lax.ppermute(theirs, "c", shift(2, 1))

    own, back = pl.pallas_call(
        functools.partial(product_kernel, [p.shape[0] for p in pieces]),
        out_shape=[jax.ShapeDtypeStruct((pairs, columns), jnp.float32)] * 2,
        in_specs=[VMEM] * (2 + len(pieces)),
        out_specs=[VMEM] * 2,
        scratch_shapes=[pltpu.VMEM((slab // 2, columns), jnp.bfloat16)] * 2,
        compiler_params=pltpu.CompilerParams(vmem_limit_bytes=16 * 2**20),
        cost_estimate=pl.CostEstimate(flops=6 * pairs * slab * columns, bytes_accessed=8 * 2**20, transcendentals=0),
        name="product",
    )(mine, theirs, *pieces)
    back = lax.ppermute(back, "c", shift(2, 1))
    weight = jnp.where(pair_list[:, 0] == pair_list[:, 1], 0.5, 1.0).astype(jnp.float32)
    return weight[:, None] * (own + back)


def solution(mesh):
    fine = Mesh(mesh.devices.reshape(4, 4, 2, 4, 4), OCC + VIR)
    placed = (P(OCC, VIR), P(OCC, VIR), P(OCC, None), P())
    return jax.shard_map(
        body, mesh=fine, in_specs=placed, out_specs=P(OCC, VIR), check_vma=False
    )
```

```python
import functools

import jax
import jax.numpy as jnp
from jax import lax
from jax.experimental import pallas as pl
from jax.experimental.pallas import tpu as pltpu
from jax.sharding import Mesh, PartitionSpec as P

NA = 128
VIR = ("y", "zh")
OCC = ("zl", "x", "c")
RING = (0, 1, 3, 2)
SLOT = (0, 2, 3, 1)
VMEM = pl.BlockSpec(memory_space=pltpu.VMEM)
SMEM = pl.BlockSpec(memory_space=pltpu.SMEM)


def shift(n, by):
    return [(i, (i + by) % n) for i in range(n)]


def pack_kernel(turned_ref, packed_ref):
    rows, pairs = turned_ref.shape
    tail = pairs - 128
    step = packed_ref.shape[0] - rows
    packed_ref[:rows, :] = turned_ref[:, :128]
    parts = [turned_ref[j : j + step, 128:] for j in range(0, rows, step)]
    parts.append(jnp.zeros((step, 128 - tail * len(parts)), jnp.float32))
    packed_ref[rows:, :] = jnp.concatenate(parts, axis=1)


def symmetrize_kernel(integrals_ref, got_ref, out_ref, turned_ref):
    ranks, here = got_ref.shape[0], integrals_ref.shape[1] // NA
    rows = integrals_ref.shape[0]
    for t in range(here * rows // 128):
        block = got_ref[:, t * here : (t + 1) * here, :].reshape(ranks * here, 128)
        turned_ref[t * 128 : (t + 1) * 128, :] = block.T
    for a in range(here):
        columns = slice(a * NA, (a + 1) * NA)
        out_ref[:, columns] = integrals_ref[:, columns] + turned_ref[a * rows : (a + 1) * rows, :]


def copies_kernel(*refs):
    copies_ref = refs[-1]
    at = 0
    for piece in refs[:-1]:
        for i in range(copies_ref.shape[0]):
            copies_ref[i, at : at + piece.shape[0], :] = piece[...]
        at += piece.shape[0]


def antisym_kernel(block, columns_k, chunk_ref, base_ref, other_ref, tau_ref, mine_ref, theirs_ref, head_ref, tail_ref, rows_ref, ends_ref):
    total = rows_ref.shape[0]
    pairs = mine_ref.shape[0]
    ranks = total // columns_k
    per = tau_ref.shape[0] // ranks
    step = per - columns_k
    for r in range(ranks):
        head_ref[r * columns_k : (r + 1) * columns_k, :] = tau_ref[r * per : r * per + columns_k, :]
        packed = tau_ref[r * per + columns_k : (r + 1) * per, :]
        for j in range(columns_k // step):
            turned = packed if j == 0 else pltpu.roll(packed, 128 - j * (pairs - 128), 1)
            tail_ref[r * columns_k + j * step : r * columns_k + (j + 1) * step, :] = turned

    def one(b, _):
        at = pl.multiple_of(b * block, 8)
        first = chunk_ref[b]
        for r in range(block):
            k = other_ref[first + r]
            rows_ref[pl.ds(at + r, 1), :] = head_ref[pl.ds(k, 1), :]
            ends_ref[pl.ds(at + r, 1), :] = tail_ref[pl.ds(k, 1), :]
        here = pl.ds(pl.multiple_of(base_ref[b], 8), block)
        rows_ref[pl.ds(at, block), :] = head_ref[here, :] - rows_ref[pl.ds(at, block), :]
        ends_ref[pl.ds(at, block), :] = tail_ref[here, :] - ends_ref[pl.ds(at, block), :]
        return 0

    lax.fori_loop(0, total // block, one, 0)
    half = total // 2
    for j in range(0, half, 128):
        mine_ref[:128, j : j + 128] = rows_ref[j : j + 128, :].T
        mine_ref[128:, j : j + 128] = ends_ref[j : j + 128, :].T[: pairs - 128]
        theirs_ref[:128, j : j + 128] = rows_ref[half + j : half + j + 128, :].T
        theirs_ref[128:, j : j + 128] = ends_ref[half + j : half + j + 128, :].T[: pairs - 128]


def product_kernel(first, counts, mine_ref, theirs_ref, *refs):
    pieces, sums = refs[: len(counts)], refs[len(counts) : -4]
    own_ref, other_ref, high_ref, low_ref = refs[-4:]
    at = 0
    for piece, count in zip(pieces, counts):
        for r in range(0, count, 80):
            value = piece[r : r + 80, :]
            high = value.astype(jnp.bfloat16)
            high_ref[at : at + 80, :] = high
            low_ref[at : at + 80, :] = (value - high.astype(jnp.float32)).astype(jnp.bfloat16)
            at += 80
    lhs = jnp.concatenate([mine_ref[:, first : first + at], theirs_ref[:, first : first + at]], axis=0)
    lhs_high = lhs.astype(jnp.bfloat16)
    lhs_low = (lhs - lhs_high.astype(jnp.float32)).astype(jnp.bfloat16)
    dot = functools.partial(jnp.dot, preferred_element_type=jnp.float32)
    pairs = own_ref.shape[0]
    for n in range(0, own_ref.shape[1], 256):
        high, low = high_ref[:, n : n + 256], low_ref[:, n : n + 256]
        total = dot(lhs_high, high) + (dot(lhs_high, low) + dot(lhs_low, high))
        if sums:
            total = total + jnp.concatenate([ref[:, n : n + 256] for ref in sums], axis=0)
        own_ref[:, n : n + 256] = total[:pairs]
        other_ref[:, n : n + 256] = total[pairs:]


def around(up, down, axis):
    return lax.ppermute(up, axis, shift(4, 1)), lax.ppermute(down, axis, shift(4, -1))


def body(amplitudes, integrals, pair_list, partner):
    rows_k, columns = integrals.shape
    pairs, columns_k = amplitudes.shape
    slab = partner.shape[0]
    x, core, zh = lax.axis_index("x"), lax.axis_index("c"), lax.axis_index("zh")
    ring_place = jnp.array([0, 1, 3, 2], jnp.int32)[lax.axis_index("zl")]

    lanes = 128 // (pairs - 128)
    packed_rows = columns_k + columns_k // lanes
    packed = pl.pallas_call(
        pack_kernel,
        out_shape=jax.ShapeDtypeStruct((packed_rows, 128), jnp.float32),
        in_specs=[VMEM],
        out_specs=VMEM,
        compiler_params=pltpu.CompilerParams(vmem_limit_bytes=8 * 2**20),
        name="pack",
    )(amplitudes.T)
    left, right = around(packed, packed, "zh")
    half = packed_rows // 2
    far = around(left[:half], right[half:], "zh")
    copies = pl.pallas_call(
        copies_kernel,
        out_shape=jax.ShapeDtypeStruct((4, 4 * packed_rows, 128), jnp.float32),
        in_specs=[VMEM] * 5,
        out_specs=VMEM,
        compiler_params=pltpu.CompilerParams(vmem_limit_bytes=8 * 2**20),
        name="copies",
    )(packed, left, right, *far)
    tau = lax.all_to_all(copies, "y", split_axis=0, concat_axis=0, tiled=True).reshape(-1, 128)

    here = columns // NA
    ranks = NA // here
    tiles = here * rows_k // 128
    blocks = integrals.reshape(rows_k, here, ranks, here).transpose(2, 1, 3, 0).reshape(ranks, here, tiles, 128)
    sent = blocks.transpose(0, 2, 1, 3).reshape(ranks, tiles * here, 128)
    got = lax.all_to_all(sent, VIR, split_axis=0, concat_axis=0, tiled=True)
    start = pl.pallas_call(
        symmetrize_kernel,
        out_shape=jax.ShapeDtypeStruct((rows_k, columns), jnp.float32),
        in_specs=[VMEM] * 2,
        out_specs=VMEM,
        scratch_shapes=[pltpu.VMEM((tiles * 128, 128), jnp.float32)],
        compiler_params=pltpu.CompilerParams(vmem_limit_bytes=8 * 2**20),
        name="symmetrize",
    )(integrals, got)

    def lower(block):
        return lax.ppermute(block, "zl", [(RING[i], RING[(i + 1) % 4]) for i in range(4)])

    one = lower(start)
    two = lower(one)
    first = jnp.concatenate([start, one], axis=0)
    first = [first, *around(first, first, "x")]
    three = lower(two)
    last = jnp.concatenate([two, three], axis=0)
    last = [last, *around(last, last, "x")]
    pieces, order = [], []
    for i, part in ((0, first), (2, last)):
        pieces += part + [lax.ppermute(part[1 + i // 2], "x", shift(4, 1 - i))]
        order += [(i, 0), (i + 1, 0), (i, -1), (i + 1, -1), (i, 1), (i + 1, 1), (i, 2), (i + 1, 2)]

    pieces[1:4], tau = lax.optimization_barrier((pieces[1:4], tau))

    slot = jnp.array(SLOT, jnp.int32)

    def place(k):
        rank = k // columns_k
        return k + (slot[(rank % 4 - zh) % 4] - rank % 4) * columns_k

    steps = jnp.array(order, jnp.int32)
    zs = jnp.array(RING, jnp.int32)[(ring_place - steps[:, 0]) % 4]
    chunk = (zs * 4 + (x + steps[:, 1]) % 4) * 2
    chunk = jnp.concatenate([chunk + core, chunk + 1 - core]) * rows_k
    mine, theirs = pl.pallas_call(
        functools.partial(antisym_kernel, rows_k, columns_k),
        out_shape=[jax.ShapeDtypeStruct((pairs, slab // 2), jnp.float32)] * 2,
        in_specs=[SMEM, SMEM, SMEM, VMEM],
        out_specs=[VMEM] * 2,
        scratch_shapes=[pltpu.VMEM((slab, 128), jnp.float32)] * 4,
        compiler_params=pltpu.CompilerParams(vmem_limit_bytes=10 * 2**20),
        cost_estimate=pl.CostEstimate(flops=slab * pairs, bytes_accessed=3 * slab * pairs * 4, transcendentals=0),
        name="antisym",
    )(chunk, place(chunk), place(partner), tau)
    theirs = lax.ppermute(theirs, "c", shift(2, 1))

    def product(first, pieces, sums):
        return pl.pallas_call(
            functools.partial(product_kernel, first, [p.shape[0] for p in pieces]),
            out_shape=[jax.ShapeDtypeStruct((pairs, columns), jnp.float32)] * 2,
            in_specs=[VMEM] * (2 + len(pieces) + len(sums)),
            out_specs=[VMEM] * 2,
            scratch_shapes=[pltpu.VMEM((slab // 4, columns), jnp.bfloat16)] * 2,
            compiler_params=pltpu.CompilerParams(vmem_limit_bytes=16 * 2**20),
            cost_estimate=pl.CostEstimate(flops=3 * pairs * slab * columns, bytes_accessed=4 * 2**20, transcendentals=0),
            name="product",
        )(mine, theirs, *pieces, *sums)

    own, back = product(slab // 4, pieces[4:], product(0, pieces[:4], ()))
    back = lax.ppermute(back, "c", shift(2, 1))
    weight = jnp.where(pair_list[:, 0] == pair_list[:, 1], 0.5, 1.0).astype(jnp.float32)
    return weight[:, None] * (own + back)


def solution(mesh):
    fine = Mesh(mesh.devices.reshape(4, 4, 2, 4, 4), OCC + VIR)
    placed = (P(OCC, VIR), P(OCC, VIR), P(OCC, None), P())
    return jax.shard_map(
        body, mesh=fine, in_specs=placed, out_specs=P(OCC, VIR), check_vma=False
    )
```

```python
import functools

import jax
import jax.numpy as jnp
from jax import lax
from jax.experimental import pallas as pl
from jax.experimental.pallas import tpu as pltpu
from jax.sharding import Mesh, PartitionSpec as P

NA = 128
VIR = ("y", "zh")
OCC = ("zl", "x", "c")
RING = (0, 1, 3, 2)
SLOT = (0, 2, 3, 1)
VMEM = pl.BlockSpec(memory_space=pltpu.VMEM)
SMEM = pl.BlockSpec(memory_space=pltpu.SMEM)


def shift(n, by):
    return [(i, (i + by) % n) for i in range(n)]


def pack_kernel(turned_ref, packed_ref):
    rows, pairs = turned_ref.shape
    tail = pairs - 128
    step = packed_ref.shape[0] - rows
    packed_ref[:rows, :] = turned_ref[:, :128]
    parts = [turned_ref[j : j + step, 128:] for j in range(0, rows, step)]
    parts.append(jnp.zeros((step, 128 - tail * len(parts)), jnp.float32))
    packed_ref[rows:, :] = jnp.concatenate(parts, axis=1)


def symmetrize_kernel(integrals_ref, got_ref, out_ref, turned_ref):
    ranks, here = got_ref.shape[0], integrals_ref.shape[1] // NA
    rows = integrals_ref.shape[0]
    for t in range(here * rows // 128):
        block = got_ref[:, t * here : (t + 1) * here, :].reshape(ranks * here, 128)
        turned_ref[t * 128 : (t + 1) * 128, :] = block.T
    for a in range(here):
        columns = slice(a * NA, (a + 1) * NA)
        out_ref[:, columns] = integrals_ref[:, columns] + turned_ref[a * rows : (a + 1) * rows, :]


def copies_kernel(*refs):
    copies_ref = refs[-1]
    at = 0
    for piece in refs[:-1]:
        for i in range(copies_ref.shape[0]):
            copies_ref[i, at : at + piece.shape[0], :] = piece[...]
        at += piece.shape[0]


def antisym_kernel(block, columns_k, chunk_ref, base_ref, other_ref, tau_ref, mine_ref, theirs_ref, head_ref, tail_ref, rows_ref, ends_ref):
    total = rows_ref.shape[0]
    pairs = mine_ref.shape[0]
    ranks = total // columns_k
    per = tau_ref.shape[0] // ranks
    step = per - columns_k
    for r in range(ranks):
        head_ref[r * columns_k : (r + 1) * columns_k, :] = tau_ref[r * per : r * per + columns_k, :]
        packed = tau_ref[r * per + columns_k : (r + 1) * per, :]
        for j in range(columns_k // step):
            turned = packed if j == 0 else pltpu.roll(packed, 128 - j * (pairs - 128), 1)
            tail_ref[r * columns_k + j * step : r * columns_k + (j + 1) * step, :] = turned

    def one(b, _):
        at = pl.multiple_of(b * block, 8)
        first = chunk_ref[b]
        for r in range(block):
            k = other_ref[first + r]
            rows_ref[pl.ds(at + r, 1), :] = head_ref[pl.ds(k, 1), :]
            ends_ref[pl.ds(at + r, 1), :] = tail_ref[pl.ds(k, 1), :]
        here = pl.ds(pl.multiple_of(base_ref[b], 8), block)
        rows_ref[pl.ds(at, block), :] = head_ref[here, :] - rows_ref[pl.ds(at, block), :]
        ends_ref[pl.ds(at, block), :] = tail_ref[here, :] - ends_ref[pl.ds(at, block), :]
        return 0

    lax.fori_loop(0, total // block, one, 0)
    half = total // 2
    for j in range(0, half, 128):
        mine_ref[:128, j : j + 128] = rows_ref[j : j + 128, :].T
        mine_ref[128:, j : j + 128] = ends_ref[j : j + 128, :].T[: pairs - 128]
        theirs_ref[:128, j : j + 128] = rows_ref[half + j : half + j + 128, :].T
        theirs_ref[128:, j : j + 128] = ends_ref[half + j : half + j + 128, :].T[: pairs - 128]


def product_kernel(first, counts, mine_ref, theirs_ref, *refs):
    pieces, sums = refs[: len(counts)], refs[len(counts) : -4]
    own_ref, other_ref, high_ref, low_ref = refs[-4:]
    at = 0
    for piece, count in zip(pieces, counts):
        for r in range(0, count, 80):
            value = piece[r : r + 80, :]
            high = value.astype(jnp.bfloat16)
            high_ref[at : at + 80, :] = high
            low_ref[at : at + 80, :] = (value - high.astype(jnp.float32)).astype(jnp.bfloat16)
            at += 80
    lhs = jnp.concatenate([mine_ref[:, first : first + at], theirs_ref[:, first : first + at]], axis=0)
    lhs_high = lhs.astype(jnp.bfloat16)
    lhs_low = (lhs - lhs_high.astype(jnp.float32)).astype(jnp.bfloat16)
    dot = functools.partial(jnp.dot, preferred_element_type=jnp.float32)
    pairs = own_ref.shape[0]
    for n in range(0, own_ref.shape[1], 256):
        high, low = high_ref[:, n : n + 256], low_ref[:, n : n + 256]
        total = dot(lhs_high, high) + (dot(lhs_high, low) + dot(lhs_low, high))
        if sums:
            total = total + jnp.concatenate([ref[:, n : n + 256] for ref in sums], axis=0)
        own_ref[:, n : n + 256] = total[:pairs]
        other_ref[:, n : n + 256] = total[pairs:]


def around(up, down, axis):
    return lax.ppermute(up, axis, shift(4, 1)), lax.ppermute(down, axis, shift(4, -1))


def body(amplitudes, integrals, pair_list, partner):
    rows_k, columns = integrals.shape
    pairs, columns_k = amplitudes.shape
    slab = partner.shape[0]
    x, core, zh = lax.axis_index("x"), lax.axis_index("c"), lax.axis_index("zh")
    ring_place = jnp.array([0, 1, 3, 2], jnp.int32)[lax.axis_index("zl")]

    lanes = 128 // (pairs - 128)
    packed_rows = columns_k + columns_k // lanes
    packed = pl.pallas_call(
        pack_kernel,
        out_shape=jax.ShapeDtypeStruct((packed_rows, 128), jnp.float32),
        in_specs=[VMEM],
        out_specs=VMEM,
        compiler_params=pltpu.CompilerParams(vmem_limit_bytes=8 * 2**20),
        name="pack",
    )(amplitudes.T)
    left, right = around(packed, packed, "zh")
    half = packed_rows // 2
    far = around(left[:half], right[half:], "zh")
    copies = pl.pallas_call(
        copies_kernel,
        out_shape=jax.ShapeDtypeStruct((4, 4 * packed_rows, 128), jnp.float32),
        in_specs=[VMEM] * 5,
        out_specs=VMEM,
        compiler_params=pltpu.CompilerParams(vmem_limit_bytes=8 * 2**20),
        name="copies",
    )(packed, left, right, *far)
    tau = lax.all_to_all(copies, "y", split_axis=0, concat_axis=0, tiled=True).reshape(-1, 128)

    here = columns // NA
    ranks = NA // here
    tiles = here * rows_k // 128
    blocks = integrals.reshape(rows_k, here, ranks, here).transpose(2, 1, 3, 0).reshape(ranks, here, tiles, 128)
    sent = blocks.transpose(0, 2, 1, 3).reshape(ranks, tiles * here, 128)
    got = lax.all_to_all(sent, VIR, split_axis=0, concat_axis=0, tiled=True)
    start = pl.pallas_call(
        symmetrize_kernel,
        out_shape=jax.ShapeDtypeStruct((rows_k, columns), jnp.float32),
        in_specs=[VMEM] * 2,
        out_specs=VMEM,
        scratch_shapes=[pltpu.VMEM((tiles * 128, 128), jnp.float32)],
        compiler_params=pltpu.CompilerParams(vmem_limit_bytes=8 * 2**20),
        name="symmetrize",
    )(integrals, got)

    def lower(block):
        return lax.ppermute(block, "zl", [(RING[i], RING[(i + 1) % 4]) for i in range(4)])

    one = lower(start)
    two = lower(one)
    first = jnp.concatenate([start, one], axis=0)
    first = [first, *around(first, first, "x")]
    three = lower(two)
    last = jnp.concatenate([two, three], axis=0)
    last = [last, *around(last, last, "x")]
    pieces, order = [], []
    for i, part in ((0, first), (2, last)):
        pieces += part + [lax.ppermute(part[1 + i // 2], "x", shift(4, 1 - i))]
        order += [(i, 0), (i + 1, 0), (i, -1), (i + 1, -1), (i, 1), (i + 1, 1), (i, 2), (i + 1, 2)]

    pieces[1:4], tau = lax.optimization_barrier((pieces[1:4], tau))

    slot = jnp.array(SLOT, jnp.int32)

    def place(k):
        rank = k // columns_k
        return k + (slot[(rank % 4 - zh) % 4] - rank % 4) * columns_k

    steps = jnp.array(order, jnp.int32)
    zs = jnp.array(RING, jnp.int32)[(ring_place - steps[:, 0]) % 4]
    chunk = (zs * 4 + (x + steps[:, 1]) % 4) * 2
    chunk = jnp.concatenate([chunk + core, chunk + 1 - core]) * rows_k
    mine, theirs = pl.pallas_call(
        functools.partial(antisym_kernel, rows_k, columns_k),
        out_shape=[jax.ShapeDtypeStruct((pairs, slab // 2), jnp.float32)] * 2,
        in_specs=[SMEM, SMEM, SMEM, VMEM],
        out_specs=[VMEM] * 2,
        scratch_shapes=[pltpu.VMEM((slab, 128), jnp.float32)] * 4,
        compiler_params=pltpu.CompilerParams(vmem_limit_bytes=10 * 2**20),
        cost_estimate=pl.CostEstimate(flops=slab * pairs, bytes_accessed=slab * pairs * 64, transcendentals=0),
        name="antisym",
    )(chunk, place(chunk), place(partner), tau)
    theirs = lax.ppermute(theirs, "c", shift(2, 1))

    def product(first, pieces, sums):
        return pl.pallas_call(
            functools.partial(product_kernel, first, [p.shape[0] for p in pieces]),
            out_shape=[jax.ShapeDtypeStruct((pairs, columns), jnp.float32)] * 2,
            in_specs=[VMEM] * (2 + len(pieces) + len(sums)),
            out_specs=[VMEM] * 2,
            scratch_shapes=[pltpu.VMEM((slab // 4, columns), jnp.bfloat16)] * 2,
            compiler_params=pltpu.CompilerParams(vmem_limit_bytes=16 * 2**20),
            cost_estimate=pl.CostEstimate(flops=pairs * slab * columns, bytes_accessed=2**20, transcendentals=0),
            name="product",
        )(mine, theirs, *pieces, *sums)

    own, back = product(slab // 4, pieces[4:], product(0, pieces[:4], ()))
    back = lax.ppermute(back, "c", shift(2, 1))
    weight = jnp.where(pair_list[:, 0] == pair_list[:, 1], 0.5, 1.0).astype(jnp.float32)
    return weight[:, None] * (own + back)


def solution(mesh):
    fine = Mesh(mesh.devices.reshape(4, 4, 2, 4, 4), OCC + VIR)
    placed = (P(OCC, VIR), P(OCC, VIR), P(OCC, None), P())
    return jax.shard_map(
        body, mesh=fine, in_specs=placed, out_specs=P(OCC, VIR), check_vma=False
    )
```

```python
import functools

import jax
import jax.numpy as jnp
from jax import lax
from jax.experimental import pallas as pl
from jax.experimental.pallas import tpu as pltpu
from jax.sharding import Mesh, PartitionSpec as P

NA = 128
VIR = ("y", "zh")
OCC = ("zl", "x", "c")
RING = (0, 1, 3, 2)
SLOT = (0, 2, 3, 1)
VMEM = pl.BlockSpec(memory_space=pltpu.VMEM)
SMEM = pl.BlockSpec(memory_space=pltpu.SMEM)


def shift(n, by):
    return [(i, (i + by) % n) for i in range(n)]


def pack_kernel(turned_ref, packed_ref):
    rows, pairs = turned_ref.shape
    tail = pairs - 128
    step = packed_ref.shape[0] - rows
    packed_ref[:rows, :] = turned_ref[:, :128]
    parts = [turned_ref[j : j + step, 128:] for j in range(0, rows, step)]
    parts.append(jnp.zeros((step, 128 - tail * len(parts)), jnp.float32))
    packed_ref[rows:, :] = jnp.concatenate(parts, axis=1)


def symmetrize_kernel(integrals_ref, got_ref, out_ref, turned_ref):
    ranks, here = got_ref.shape[0], integrals_ref.shape[1] // NA
    rows = integrals_ref.shape[0]
    for t in range(here * rows // 128):
        block = got_ref[:, t * here : (t + 1) * here, :].reshape(ranks * here, 128)
        turned_ref[t * 128 : (t + 1) * 128, :] = block.T
    for a in range(here):
        columns = slice(a * NA, (a + 1) * NA)
        out_ref[:, columns] = integrals_ref[:, columns] + turned_ref[a * rows : (a + 1) * rows, :]


def copies_kernel(*refs):
    copies_ref = refs[-1]
    at = 0
    for piece in refs[:-1]:
        for i in range(copies_ref.shape[0]):
            copies_ref[i, at : at + piece.shape[0], :] = piece[...]
        at += piece.shape[0]


def antisym_kernel(block, columns_k, chunk_ref, base_ref, other_ref, tau_ref, mine_ref, theirs_ref, head_ref, tail_ref, rows_ref, ends_ref):
    total = rows_ref.shape[0]
    pairs = mine_ref.shape[0]
    ranks = total // columns_k
    per = tau_ref.shape[0] // ranks
    step = per - columns_k
    for r in range(ranks):
        head_ref[r * columns_k : (r + 1) * columns_k, :] = tau_ref[r * per : r * per + columns_k, :]
        packed = tau_ref[r * per + columns_k : (r + 1) * per, :]
        for j in range(columns_k // step):
            turned = packed if j == 0 else pltpu.roll(packed, 128 - j * (pairs - 128), 1)
            tail_ref[r * columns_k + j * step : r * columns_k + (j + 1) * step, :] = turned

    def one(b, _):
        at = pl.multiple_of(b * block, 8)
        first = chunk_ref[b]
        for r in range(block):
            k = other_ref[first + r]
            rows_ref[pl.ds(at + r, 1), :] = head_ref[pl.ds(k, 1), :]
            ends_ref[pl.ds(at + r, 1), :] = tail_ref[pl.ds(k, 1), :]
        here = pl.ds(pl.multiple_of(base_ref[b], 8), block)
        rows_ref[pl.ds(at, block), :] = head_ref[here, :] - rows_ref[pl.ds(at, block), :]
        ends_ref[pl.ds(at, block), :] = tail_ref[here, :] - ends_ref[pl.ds(at, block), :]
        return 0

    lax.fori_loop(0, total // block, one, 0)
    half = total // 2
    for j in range(0, half, 128):
        mine_ref[:128, j : j + 128] = rows_ref[j : j + 128, :].T
        mine_ref[128:, j : j + 128] = ends_ref[j : j + 128, :].T[: pairs - 128]
        theirs_ref[:128, j : j + 128] = rows_ref[half + j : half + j + 128, :].T
        theirs_ref[128:, j : j + 128] = ends_ref[half + j : half + j + 128, :].T[: pairs - 128]


def product_kernel(first, counts, mine_ref, theirs_ref, *refs):
    pieces, sums = refs[: len(counts)], refs[len(counts) : -4]
    own_ref, other_ref, high_ref, low_ref = refs[-4:]
    at = 0
    for piece, count in zip(pieces, counts):
        for r in range(0, count, 80):
            value = piece[r : r + 80, :]
            high = value.astype(jnp.bfloat16)
            high_ref[at : at + 80, :] = high
            low_ref[at : at + 80, :] = (value - high.astype(jnp.float32)).astype(jnp.bfloat16)
            at += 80
    lhs = jnp.concatenate([mine_ref[:, first : first + at], theirs_ref[:, first : first + at]], axis=0)
    lhs_high = lhs.astype(jnp.bfloat16)
    lhs_low = (lhs - lhs_high.astype(jnp.float32)).astype(jnp.bfloat16)
    dot = functools.partial(jnp.dot, preferred_element_type=jnp.float32)
    pairs = own_ref.shape[0]
    for n in range(0, own_ref.shape[1], 256):
        high, low = high_ref[:, n : n + 256], low_ref[:, n : n + 256]
        total = dot(lhs_high, high) + (dot(lhs_high, low) + dot(lhs_low, high))
        if sums:
            total = total + jnp.concatenate([ref[:, n : n + 256] for ref in sums], axis=0)
        own_ref[:, n : n + 256] = total[:pairs]
        other_ref[:, n : n + 256] = total[pairs:]


def around(up, down, axis):
    return lax.ppermute(up, axis, shift(4, 1)), lax.ppermute(down, axis, shift(4, -1))


def body(amplitudes, integrals, pair_list, partner):
    rows_k, columns = integrals.shape
    pairs, columns_k = amplitudes.shape
    slab = partner.shape[0]
    x, core, zh = lax.axis_index("x"), lax.axis_index("c"), lax.axis_index("zh")
    ring_place = jnp.array([0, 1, 3, 2], jnp.int32)[lax.axis_index("zl")]

    lanes = 128 // (pairs - 128)
    packed_rows = columns_k + columns_k // lanes
    packed = pl.pallas_call(
        pack_kernel,
        out_shape=jax.ShapeDtypeStruct((packed_rows, 128), jnp.float32),
        in_specs=[VMEM],
        out_specs=VMEM,
        compiler_params=pltpu.CompilerParams(vmem_limit_bytes=8 * 2**20),
        name="pack",
    )(amplitudes.T)
    left, right = around(packed, packed, "zh")
    half = packed_rows // 2
    far = around(left[:half], right[half:], "zh")
    copies = pl.pallas_call(
        copies_kernel,
        out_shape=jax.ShapeDtypeStruct((4, 4 * packed_rows, 128), jnp.float32),
        in_specs=[VMEM] * 5,
        out_specs=VMEM,
        compiler_params=pltpu.CompilerParams(vmem_limit_bytes=8 * 2**20),
        name="copies",
    )(packed, left, right, *far)
    tau = lax.all_to_all(copies, "y", split_axis=0, concat_axis=0, tiled=True).reshape(-1, 128)

    here = columns // NA
    ranks = NA // here
    tiles = here * rows_k // 128
    blocks = integrals.reshape(rows_k, here, ranks, here).transpose(2, 1, 3, 0).reshape(ranks, here, tiles, 128)
    sent = blocks.transpose(0, 2, 1, 3).reshape(ranks, tiles * here, 128)
    got = lax.all_to_all(sent, VIR, split_axis=0, concat_axis=0, tiled=True)
    start = pl.pallas_call(
        symmetrize_kernel,
        out_shape=jax.ShapeDtypeStruct((rows_k, columns), jnp.float32),
        in_specs=[VMEM] * 2,
        out_specs=VMEM,
        scratch_shapes=[pltpu.VMEM((tiles * 128, 128), jnp.float32)],
        compiler_params=pltpu.CompilerParams(vmem_limit_bytes=8 * 2**20),
        name="symmetrize",
    )(integrals, got)

    def lower(block):
        return lax.ppermute(block, "zl", [(RING[i], RING[(i + 1) % 4]) for i in range(4)])

    one = lower(start)
    two = lower(one)
    first = jnp.concatenate([start, one], axis=0)
    first = [first, *around(first, first, "x")]
    three = lower(two)
    last = jnp.concatenate([two, three], axis=0)
    last = [last, *around(last, last, "x")]
    pieces, order = [], []
    for i, part in ((0, first), (2, last)):
        pieces += part + [lax.ppermute(part[1 + i // 2], "x", shift(4, 1 - i))]
        order += [(i, 0), (i + 1, 0), (i, -1), (i + 1, -1), (i, 1), (i + 1, 1), (i, 2), (i + 1, 2)]

    pieces[1:4], tau = lax.optimization_barrier((pieces[1:4], tau))

    slot = jnp.array(SLOT, jnp.int32)

    def place(k):
        rank = k // columns_k
        return k + (slot[(rank % 4 - zh) % 4] - rank % 4) * columns_k

    steps = jnp.array(order, jnp.int32)
    zs = jnp.array(RING, jnp.int32)[(ring_place - steps[:, 0]) % 4]
    chunk = (zs * 4 + (x + steps[:, 1]) % 4) * 2
    chunk = jnp.concatenate([chunk + core, chunk + 1 - core]) * rows_k
    mine, theirs = pl.pallas_call(
        functools.partial(antisym_kernel, rows_k, columns_k),
        out_shape=[jax.ShapeDtypeStruct((pairs, slab // 2), jnp.float32)] * 2,
        in_specs=[SMEM, SMEM, SMEM, VMEM],
        out_specs=[VMEM] * 2,
        scratch_shapes=[pltpu.VMEM((slab, 128), jnp.float32)] * 4,
        compiler_params=pltpu.CompilerParams(vmem_limit_bytes=10 * 2**20),
        cost_estimate=pl.CostEstimate(flops=slab * pairs, bytes_accessed=3 * slab * pairs * 4, transcendentals=0),
        name="antisym",
    )(chunk, place(chunk), place(partner), tau)
    theirs = lax.ppermute(theirs, "c", shift(2, 1))

    def product(first, pieces, sums):
        return pl.pallas_call(
            functools.partial(product_kernel, first, [p.shape[0] for p in pieces]),
            out_shape=[jax.ShapeDtypeStruct((pairs, columns), jnp.float32)] * 2,
            in_specs=[VMEM] * (2 + len(pieces) + len(sums)),
            out_specs=[VMEM] * 2,
            scratch_shapes=[pltpu.VMEM((slab // 4, columns), jnp.bfloat16)] * 2,
            compiler_params=pltpu.CompilerParams(vmem_limit_bytes=12 * 2**20),
            cost_estimate=pl.CostEstimate(flops=3 * pairs * slab * columns, bytes_accessed=4 * 2**20, transcendentals=0),
            name="product",
        )(mine, theirs, *pieces, *sums)

    own, back = product(slab // 4, pieces[4:], product(0, pieces[:4], ()))
    back = lax.ppermute(back, "c", shift(2, 1))
    weight = jnp.where(pair_list[:, 0] == pair_list[:, 1], 0.5, 1.0).astype(jnp.float32)
    return weight[:, None] * (own + back)


def solution(mesh):
    fine = Mesh(mesh.devices.reshape(4, 4, 2, 4, 4), OCC + VIR)
    placed = (P(OCC, VIR), P(OCC, VIR), P(OCC, None), P())
    return jax.shard_map(
        body, mesh=fine, in_specs=placed, out_specs=P(OCC, VIR), check_vma=False
    )
```
